512 devices in a mesh: expert: 64 (over y, z), width: 8 (over x, core).
Axes of the slice: x: 4, y: 4, z: 16, core: 2. Of those that a mesh axis runs over, the one named last changes fastest.
Arguments:
- tokens: bfloat16 [4096, 6144], P('expert', 'width'), may hold values from -6 to 6
- expert_ids: int32 [4096, 8], P('expert'), may hold values from 0 to 383, all different within a row; in each aligned block of 64 rows (0 to 63, 64 to 127, ...) at most 2 rows name the same one
- route_weight: float32 [4096, 8], P('expert'), may hold values from 0.2 to 1.5
- gate_weight: bfloat16 [64, 6144, 1024], P('expert', None, 'width'), may hold values from -0.078125 to 0.078125
- up_weight: bfloat16 [64, 6144, 1024], P('expert', None, 'width'), may hold values from -0.078125 to 0.078125
- down_weight: bfloat16 [64, 6144, 1024], P('expert', None, 'width'), may hold values from -0.1875 to 0.1875
Outputs:
- mixed: bfloat16 [4096, 6144], P('expert', 'width')
The draws below stay inside these ranges and needn't reach their ends.
Inputs may be any that keep to these rules, and one draw needn't show every extreme that they name: `expert_ids`: each row names 8 different experts. In each aligned block of 64 rows (the rows of one index of the expert axis) no expert is named by more than 2 rows.
All inputs are finite; a program needn't handle non-finite values.
Results may differ from the reference program's by a relative error of at most 0.014.
Values may be sent and summed in bfloat16 or wider, within the bound.
A program may use at most 64 MiB of HBM per device.

```python
import math
import jax
import jax.numpy as jnp
import numpy as np
from jax import lax

D = 6144
FF = 1024
EXPERTS = 384
TOPK = 8
TOK_DEV = 64
SEND = 2
HELD = 64
TOKENS = 4096
N_WIDTH = 8


def block_levels(stream_key, extent, split, least, top_value):
    level, own = 1.0, jax.random.fold_in(stream_key, 6)
    for axis_at, blocks in split:
        steps = jnp.exp(jax.random.uniform(jax.random.fold_in(own, axis_at), (blocks,), jnp.float32, least / len(split), top_value / len(split)))
        level = level * jnp.repeat(steps, extent[axis_at] // blocks).reshape([-1 if axis == axis_at else 1 for axis in range(len(extent))])
    return level


def shared_out(stream_key, own, number, rows, count, top, bound, skew):
    order = jax.random.permutation(stream_key, count)
    packed, usual = load_shares(count, rows * top, bound, skew, True), load_shares(count, rows * top, bound, skew, False)
    places = jnp.arange(count)

    def named(tallies, turn):
        used = int((tallies > 0).sum())
        fixed = max(1, used // 4)
        moved = fixed + (places - fixed + turn * (used - fixed)) % max(1, count - fixed)
        return jnp.zeros((count,), jnp.int32).at[order[jnp.where(places < fixed, places, moved)]].set(jnp.asarray(tallies, jnp.int32))

    tallies = jnp.where(number % 4 == 0, named(packed, number // 4), named(usual, number - number // 4 - 1))
    mixed = jax.random.permutation(jax.random.fold_in(own, 3), count)
    source_of, taker = mixed[0:count // 2 * 2:2], mixed[1:count // 2 * 2:2]
    slack = jnp.minimum(tallies[source_of] - 1, bound - tallies[taker]) // 2
    slack = jnp.where((source_of == order[0]) | (taker == order[0]) | (tallies[taker] == 0), 0, jnp.maximum(slack, 0))
    moved = jax.random.randint(jax.random.fold_in(own, 4), (count // 2,), 0, 1 << 20) % (slack + 1)
    tallies = tallies.at[source_of].add(-moved).at[taker].add(moved)
    items = jnp.searchsorted(jnp.cumsum(tallies), jnp.arange(rows * top), side="right").astype(jnp.int32)
    table = items.reshape(top, rows).T
    table = table[jax.random.permutation(jax.random.fold_in(own, 1), rows)]
    turn = jax.random.randint(jax.random.fold_in(own, 2), (rows, 1), 0, top)
    return jnp.take_along_axis(table, (jnp.arange(top)[None, :] + turn) % top, axis=1)


def load_shares(count, total, bound, lean, full):
    loads = [(1 << 20) // math.isqrt(standing ** lean) + 1 for standing in range(1, count + 1)]
    largest = bound if full else min(bound, max(-(-total // count), total * loads[0] // sum(loads)))
    least = 1 if total - largest >= count - 1 else 0
    holding, surplus = [largest] + [least] * (count - 1), total - largest - least * (count - 1)
    while surplus > 0:
        candidates = [i for i in range(1, count) if holding[i] < largest] or [i for i in range(1, count) if holding[i] < bound]
        pool, remaining = sum([loads[i] for i in candidates]), surplus
        for i in candidates:
            more = min(bound - holding[i], max(1, remaining * loads[i] // pool), surplus)
            holding[i] = holding[i] + more
            surplus = surplus - more
    return np.array(holding)


def noise(stream_key, dims, spread, most, split=(), held_as=jnp.bfloat16):
    level = block_levels(stream_key, dims, split, -0.22, 0.18) if split else 1.0
    drawn = jax.random.normal(stream_key, dims, jnp.float32) * spread * level
    return jnp.minimum(jnp.maximum(drawn, -most), most).astype(held_as)


def setup_inputs(seed: int = 0) -> dict:
    arg_keys = jax.random.split(jax.random.key(seed), 7)
    tokens = noise(arg_keys[0], (TOKENS, D), 1.0, 6.0, ((0, 64), (1, 8)))
    expert_ids_keys = jax.random.split(jax.random.fold_in(arg_keys[1], 1), TOKENS // TOK_DEV)
    expert_ids_turns = jax.random.permutation(jax.random.fold_in(arg_keys[1], 3), TOKENS // TOK_DEV)
    expert_ids = jax.vmap(lambda own, number: shared_out(jax.random.fold_in(arg_keys[1], 2), own, number, TOK_DEV, EXPERTS, TOPK, SEND, 2))(expert_ids_keys, expert_ids_turns).reshape((TOKENS, TOPK))
    route_weight = jnp.clip(0.2 + 1.3 * jax.random.uniform(arg_keys[2], (TOKENS, TOPK), jnp.float32) ** block_levels(arg_keys[2], (TOKENS, TOPK), ((0, 64),), -0.2, 0.2), 0.2, 1.5)
    gate_weight = noise(arg_keys[3], (HELD, D, FF), D ** -0.5, 0.078125, ((0, 64), (2, 8)))
    up_weight = noise(arg_keys[4], (HELD, D, FF), D ** -0.5, 0.078125, ((0, 64), (2, 8)))
    down_weight = noise(arg_keys[5], (HELD, D, FF), FF ** -0.5, 0.1875, ((0, 64), (2, 8)))
    return {"tokens": tokens, "expert_ids": expert_ids, "route_weight": route_weight, "gate_weight": gate_weight, "up_weight": up_weight, "down_weight": down_weight}


def reference(tokens, expert_ids, route_weight, gate_weight, up_weight, down_weight):
    tokens_total = tokens.shape[0]
    capacity = HELD * SEND
    width_slice = FF // N_WIDTH
    block_count = tokens_total // TOK_DEV
    row_index = jnp.arange(tokens_total, dtype=jnp.int32)
    block_of = row_index // TOK_DEV

    def expert_step(expert, combined):
        route_hits = expert_ids == expert
        routed = jnp.any(route_hits, axis=1).astype(jnp.int32)
        blocked = routed.reshape(block_count, TOK_DEV)
        ranking = (jnp.cumsum(blocked, axis=1) - blocked).reshape(-1).astype(jnp.int32)
        slot_of = jnp.where(routed > 0, block_of * SEND + ranking, capacity).astype(jnp.int32)
        slot_table = jnp.full((capacity + 1,), tokens_total, jnp.int32).at[slot_of].set(row_index)[:capacity]
        selected = jnp.take(tokens, slot_table, axis=0, mode="fill", fill_value=0)
        gate_mat = lax.dynamic_index_in_dim(gate_weight, expert, 0, keepdims=False)
        up_mat = lax.dynamic_index_in_dim(up_weight, expert, 0, keepdims=False)
        down_mat = lax.dynamic_index_in_dim(down_weight, expert, 0, keepdims=False)
        gate_val = jnp.dot(selected, gate_mat, preferred_element_type=jnp.float32)
        up_val = jnp.dot(selected, up_mat, preferred_element_type=jnp.float32)
        hidden = (jax.nn.silu(gate_val) * up_val).astype(jnp.bfloat16)
        expert_out = jnp.zeros((capacity, D), jnp.float32)
        for section in range(N_WIDTH):
            lower = section * width_slice
            part = lax.dot_general(hidden[:, lower:lower + width_slice], down_mat[:, lower:lower + width_slice],
                                   (((1,), (1,)), ((), ())), preferred_element_type=jnp.float32)
            expert_out = expert_out + part.astype(jnp.bfloat16).astype(jnp.float32)
        coeff = jnp.sum(jnp.where(route_hits, route_weight, jnp.zeros_like(route_weight)), axis=1)
        slot_coeff = jnp.take(coeff, slot_table, mode="fill", fill_value=0.0)
        return combined.at[slot_table].add(slot_coeff[:, None] * expert_out, mode="drop")

    combined = lax.fori_loop(0, HELD, expert_step, jnp.zeros((tokens_total, D), jnp.float32))
    return combined.astype(jnp.bfloat16)
```

```python
import jax
import jax.numpy as jnp
from jax import lax
from jax.experimental import pallas as pl
from jax.experimental.pallas import tpu as pltpu
from jax.sharding import PartitionSpec as P

MESH = pl.DeviceIdType.MESH
BF16 = jnp.bfloat16
F32 = jnp.float32
Y, Z, X = 4, 16, 4
SEND = 2
SLOTS = Y * Z * SEND
TOK, FEAT, FF = 64, 768, 128
D = FEAT * X * 2
NC = 3
F = FEAT // NC
HALF = Z // 2
ROWS = SLOTS // 2


def dot(a, b, dims=((1,), (0,))):
    return lax.dot_general(a, b, (dims, ((), ())), preferred_element_type=F32)


def iota(shape, dim):
    return lax.broadcasted_iota(jnp.int32, shape, dim)


def wait_bytes(ref, sem):
    pltpu.make_async_copy(ref, ref, sem).wait()


def kernel(
    tok, ids, rw, wg_hbm, wu_hbm, wd_hbm, out,
    wgu, wd, ysend, yrecv, zsend, xall, psend, precv, opp_out, opp_in,
    nbr_out, nbr_in, sums, zsend2, zrecv2, ysend2, yrecv2,
    w_sem, y_ssem, y_rsem, z_ssem, z_rsem, g_ssem, g_rsem, p_ssem, p_rsem,
    o_ssem, o_rsem, n_ssem, n_rsem, z2_ssem, z2_rsem, y2_ssem, y2_rsem,
):
    e, w = lax.axis_index("expert"), lax.axis_index("width")
    y, z = e // Z, e % Z
    x, core = w // 2, w % 2
    partner = x * 2 + (1 - core)
    xl, xr, xo = (x + X - 1) % X, (x + 1) % X, (x + 2) % X
    left, right, oppo = xl * 2 + core, xr * 2 + core, xo * 2 + core

    def ypeer(d):
        return (y + d) % Y

    def zpeer(d):
        return (z + d) % Z

    zorder = [8, 7, 9, 6, 10, 5, 11, 4, 12, 3, 13, 2, 14, 1, 15]

    weights = [
        pltpu.make_async_copy(wg_hbm.at[0], wgu.at[:, pl.ds(0, FF)], w_sem.at[0]),
        pltpu.make_async_copy(wu_hbm.at[0], wgu.at[:, pl.ds(FF, FF)], w_sem.at[1]),
        pltpu.make_async_copy(wd_hbm.at[0], wd, w_sem.at[2]),
    ]

    bar = pltpu.get_barrier_semaphore()

    def greet(ee, ww):
        pl.semaphore_signal(bar, inc=1, device_id=(ee, ww), device_id_type=MESH)

    for d in zorder:
        greet(y * Z + zpeer(d), w)
    for d in range(1, Y):
        greet(ypeer(d) * Z + z, w)
    for ww in (left, right, partner):
        greet(e, ww)
    for copy in weights:
        copy.start()

    def remote(src, dst, ssem, rsem, ee, ww):
        pltpu.make_async_remote_copy(
            src_ref=src, dst_ref=dst, send_sem=ssem, recv_sem=rsem,
            device_id=(ee, ww), device_id_type=MESH,
        ).start()

    column = iota((TOK, SLOTS), 1)
    expert = lax.shift_right_logical(column, 1)
    match = jnp.zeros((TOK, SLOTS), F32)
    weight = jnp.zeros((TOK, SLOTS), F32)
    for k in range(ids.shape[1]):
        hit = ids[:, k : k + 1] == expert
        match = jnp.where(hit, 1.0, match)
        weight = jnp.where(hit, rw[:, k : k + 1], weight)
    earlier = jnp.where(iota((TOK, TOK), 1) < iota((TOK, TOK), 0), 1.0, 0.0).astype(BF16)
    rank = dot(earlier, match.astype(BF16))
    chosen = jnp.where(rank == (column & 1).astype(F32), match, 0.0)
    coeff = weight * chosen
    coeff_hi = coeff.astype(BF16)
    coeff_lo = (coeff - coeff_hi.astype(F32)).astype(BF16)
    outgoing = dot(chosen.astype(BF16), tok[...], ((0,), (0,)))
    for c in range(NC):
        ysend[c] = outgoing[:, c * F : (c + 1) * F].astype(BF16).reshape(Y, Z * SEND, F)

    def order(a, b):
        return (
            lax.shift_left((lax.shift_right_logical(a, 1) & 3), 5)
            + lax.shift_left(lax.shift_right_logical(a, 3), 1)
            + (a & 1)
        ) == b

    i0, i1 = iota((SLOTS, SLOTS), 0), iota((SLOTS, SLOTS), 1)
    to_z = jnp.where(order(i0, i1), 1.0, 0.0).astype(BF16)
    to_y = jnp.where(order(i1, i0), 1.0, 0.0).astype(BF16)

    pl.semaphore_wait(bar, len(zorder) + (Y - 1) + 3)

    for c in range(NC):
        for d in (2, 1, 3):
            remote(ysend.at[c, ypeer(d)], yrecv.at[c, y], y_ssem, y_rsem.at[c], ypeer(d) * Z + z, w)
        pltpu.make_async_copy(ysend.at[c, y], yrecv.at[c, y], y_rsem.at[c]).start()

    for c in range(NC):
        wait_bytes(yrecv.at[c], y_rsem.at[c])
        zsend[c] = dot(to_z, yrecv[c].reshape(SLOTS, F)).astype(BF16).reshape(Z, Y * SEND, F)
        for d in zorder:
            remote(zsend.at[c, zpeer(d)], xall.at[c, w, z], z_ssem, z_rsem.at[c], y * Z + zpeer(d), w)
        pltpu.make_async_copy(zsend.at[c, z], xall.at[c, w, z], z_rsem.at[c]).start()

    lower, upper = pl.ds(0, HALF), pl.ds(HALF, HALF)

    def give(c, ref, k, ww):
        remote(ref, ref, g_ssem, g_rsem.at[c, k], e, ww)

    def own(c):
        wait_bytes(xall.at[c, w], z_rsem.at[c])
        give(c, xall.at[c, w], 0, right)
        give(c, xall.at[c, w], 1, left)
        give(c, xall.at[c, w], 4, partner)

    def forward(c):
        wait_bytes(xall.at[c, left], g_rsem.at[c, 0])
        give(c, xall.at[c, left, lower], 2, right)
        give(c, xall.at[c, left], 5, partner)
        wait_bytes(xall.at[c, right], g_rsem.at[c, 1])
        give(c, xall.at[c, right, upper], 3, left)
        give(c, xall.at[c, right], 6, partner)

    def opposite(c):
        wait_bytes(xall.at[c, oppo, lower], g_rsem.at[c, 2])
        wait_bytes(xall.at[c, oppo, upper], g_rsem.at[c, 3])
        give(c, xall.at[c, oppo], 7, partner)

    def gathered(c):
        wait_bytes(xall.at[c, partner], g_rsem.at[c, 4])
        wait_bytes(xall.at[c, xl * 2 + 1 - core], g_rsem.at[c, 5])
        wait_bytes(xall.at[c, xr * 2 + 1 - core], g_rsem.at[c, 6])
        wait_bytes(xall.at[c, xo * 2 + 1 - core], g_rsem.at[c, 7])

    def project(c, total):
        for ww in range(2 * X):
            rows = pl.ds(ww * FEAT + c * F, F)
            total = total + dot(xall[c, ww].reshape(SLOTS, F), wgu[rows, :])
        return total

    total = jnp.zeros((SLOTS, 2 * FF), F32)
    own(0)
    forward(0)
    for c in range(NC):
        if c + 1 < NC:
            own(c + 1)
        opposite(c)
        if c + 1 < NC:
            forward(c + 1)
        gathered(c)
        if c == 0:
            weights[0].wait()
            weights[1].wait()
        total = project(c, total)
    gate, up = total[:, :FF], total[:, FF:]
    hidden = (gate / (1.0 + jnp.exp(-gate)) * up).astype(BF16)
    weights[2].wait()

    def part(c, ww):
        rows = pl.ds(pl.multiple_of(ww * FEAT + c * F, F), F)
        return dot(hidden, wd[rows, :], ((1,), (1,)))

    def to_partner(c):
        for xx in range(X):
            psend[c, xx] = part(c, xx * 2 + 1 - core).astype(BF16)
        remote(psend.at[c], precv.at[c], p_ssem, p_rsem.at[c], e, partner)

    def add_cores(c):
        wait_bytes(precv.at[c], p_rsem.at[c])
        total = part(c, oppo) + precv[c, xo].astype(F32)
        opp_out[c] = total.astype(BF16).reshape(2, ROWS, F)
        remote(opp_out.at[c, 0], opp_in.at[c, 0], o_ssem, o_rsem.at[c, 0], e, right)
        remote(opp_out.at[c, 1], opp_in.at[c, 1], o_ssem, o_rsem.at[c, 1], e, left)
        sums[c, 0] = part(c, right) + precv[c, xr].astype(F32)
        sums[c, 1] = part(c, left) + precv[c, xl].astype(F32)
        sums[c, 2] = part(c, w) + precv[c, x].astype(F32)

    def to_neighbours(c):
        a, b = pl.ds(0, ROWS), pl.ds(ROWS, ROWS)
        wait_bytes(opp_in.at[c, 0], o_rsem.at[c, 0])
        nbr_out[c, 0, a] = (sums[c, 0, a] + opp_in[c, 0].astype(F32)).astype(BF16)
        nbr_out[c, 0, b] = sums[c, 0, b].astype(BF16)
        remote(nbr_out.at[c, 0], nbr_in.at[c, 0], n_ssem, n_rsem.at[c, 0], e, right)
        wait_bytes(opp_in.at[c, 1], o_rsem.at[c, 1])
        nbr_out[c, 1, a] = sums[c, 1, a].astype(BF16)
        nbr_out[c, 1, b] = (sums[c, 1, b] + opp_in[c, 1].astype(F32)).astype(BF16)
        remote(nbr_out.at[c, 1], nbr_in.at[c, 1], n_ssem, n_rsem.at[c, 1], e, left)

    def back_z(c):
        wait_bytes(nbr_in.at[c, 0], n_rsem.at[c, 0])
        wait_bytes(nbr_in.at[c, 1], n_rsem.at[c, 1])
        total = sums[c, 2] + nbr_in[c, 0].astype(F32) + nbr_in[c, 1].astype(F32)
        zsend2[c] = total.astype(BF16).reshape(Z, Y * SEND, F)
        for d in zorder:
            remote(zsend2.at[c, zpeer(d)], zrecv2.at[c, z], z2_ssem, z2_rsem.at[c], y * Z + zpeer(d), w)
        pltpu.make_async_copy(zsend2.at[c, z], zrecv2.at[c, z], z2_rsem.at[c]).start()

    def back_y(c):
        wait_bytes(zrecv2.at[c], z2_rsem.at[c])
        ysend2[c] = dot(to_y, zrecv2[c].reshape(SLOTS, F)).astype(BF16).reshape(Y, Z * SEND, F)
        for d in (2, 1, 3):
            remote(ysend2.at[c, ypeer(d)], yrecv2.at[c, y], y2_ssem, y2_rsem.at[c], ypeer(d) * Z + z, w)
        pltpu.make_async_copy(ysend2.at[c, y], yrecv2.at[c, y], y2_rsem.at[c]).start()

    def combine(c):
        wait_bytes(yrecv2.at[c], y2_rsem.at[c])
        returned = yrecv2[c].reshape(SLOTS, F)
        mixed = dot(coeff_hi, returned) + dot(coeff_lo, returned)
        out[:, c * F : (c + 1) * F] = mixed.astype(BF16)

    steps = [to_partner, add_cores, to_neighbours, back_z, back_y, combine]
    at = [0, 1, 2.5, 4, 7, 8.5]
    plan = sorted((at[s] + 1.5 * c, s, c) for s in range(len(steps)) for c in range(NC))
    for _, s, c in plan:
        steps[s](c)

    wait_bytes(ysend.at[:, pl.ds(0, Y - 1)], y_ssem)
    wait_bytes(zsend.at[:, pl.ds(0, Z - 1)], z_ssem)
    wait_bytes(xall.at[:, pl.ds(0, 7)], g_ssem)
    wait_bytes(psend, p_ssem)
    wait_bytes(opp_out, o_ssem)
    wait_bytes(nbr_out, n_ssem)
    wait_bytes(zsend2.at[:, pl.ds(0, Z - 1)], z2_ssem)
    wait_bytes(ysend2.at[:, pl.ds(0, Y - 1)], y2_ssem)


def body(tokens, expert_ids, route_weight, gate_weight, up_weight, down_weight):
    vmem = pl.BlockSpec(memory_space=pltpu.VMEM)
    hbm = pl.BlockSpec(memory_space=pl.ANY)
    dma = pltpu.SemaphoreType.DMA
    return pl.pallas_call(
        kernel,
        out_shape=jax.ShapeDtypeStruct((TOK, FEAT), BF16),
        in_specs=[vmem, vmem, vmem, hbm, hbm, hbm],
        out_specs=vmem,
        scratch_shapes=[
            pltpu.VMEM((D, 2 * FF), BF16),
            pltpu.VMEM((D, FF), BF16),
            pltpu.VMEM((NC, Y, Z * SEND, F), BF16),
            pltpu.VMEM((NC, Y, Z * SEND, F), BF16),
            pltpu.VMEM((NC, Z, Y * SEND, F), BF16),
            pltpu.VMEM((NC, 2 * X, Z, Y * SEND, F), BF16),
            pltpu.VMEM((NC, X, SLOTS, F), BF16),
            pltpu.VMEM((NC, X, SLOTS, F), BF16),
            pltpu.VMEM((NC, 2, ROWS, F), BF16),
            pltpu.VMEM((NC, 2, ROWS, F), BF16),
            pltpu.VMEM((NC, 2, SLOTS, F), BF16),
            pltpu.VMEM((NC, 2, SLOTS, F), BF16),
            pltpu.VMEM((NC, 3, SLOTS, F), F32),
            pltpu.VMEM((NC, Z, Y * SEND, F), BF16),
            pltpu.VMEM((NC, Z, Y * SEND, F), BF16),
            pltpu.VMEM((NC, Y, Z * SEND, F), BF16),
            pltpu.VMEM((NC, Y, Z * SEND, F), BF16),
            dma((3,)),
            dma, dma((NC,)), dma, dma((NC,)), dma, dma((NC, 8)), dma, dma((NC,)),
            dma, dma((NC, 2)), dma, dma((NC, 2)), dma, dma((NC,)), dma, dma((NC,)),
        ],
        compiler_params=pltpu.CompilerParams(
            collective_id=0, has_side_effects=True, vmem_limit_bytes=40 * 2**20
        ),
        cost_estimate=pl.CostEstimate(flops=6 * SLOTS * D * FF, bytes_accessed=6 * D * FF, transcendentals=SLOTS * FF),
        name="experts",
    )(tokens, expert_ids, route_weight, gate_weight, up_weight, down_weight)


def solution(mesh):
    in_specs = (
        P("expert", "width"),
        P("expert", None),
        P("expert", None),
        P("expert", None, "width"),
        P("expert", None, "width"),
        P("expert", None, "width"),
    )
    out_specs = P("expert", "width")
    return jax.shard_map(body, mesh=mesh, in_specs=in_specs, out_specs=out_specs, check_vma=False)
```

```python
import jax
import jax.numpy as jnp
from jax import lax
from jax.experimental import pallas as pl
from jax.experimental.pallas import tpu as pltpu
from jax.sharding import PartitionSpec as P

MESH = pl.DeviceIdType.MESH
BF16 = jnp.bfloat16
F32 = jnp.float32
Y, Z, X = 4, 16, 4
TOK, FEAT, FF = 64, 768, 128
CHIP = 2 * FF
Q = 2
NF = 1
FH = FEAT // 2
F = FH // NF
SLOTS = Y * Z * 2


def dot(a, b, dims=((1,), (0,))):
    return lax.dot_general(a, b, (dims, ((), ())), preferred_element_type=F32)


def iota(shape, dim):
    return lax.broadcasted_iota(jnp.int32, shape, dim)


def shr(a, n):
    return lax.shift_right_logical(a, n)


def wait_bytes(ref, sem):
    pltpu.make_async_copy(ref, ref, sem).wait()


def kernel(
    tok, ids, rw, wg_hbm, wu_hbm, wd_hbm, out,
    wgu, wd, ysend, yrecv, zsend, xall, part, other, rsend, rrecv, mine,
    zsend2, zrecv2, ysend2, yrecv2, mixed,
    w_sem, w_ssem, w_rsem, y_ssem, y_rsem, z_ssem, z_rsem, x_ssem, x_rsem, p_ssem, p_rsem,
    r_ssem, r_rsem, z2_ssem, z2_rsem, y2_ssem, y2_rsem,
):
    e, w = lax.axis_index("expert"), lax.axis_index("width")
    y, z = e // Z, e % Z
    x, core = w // 2, w % 2
    partner = x * 2 + (1 - core)
    xl, xr, xo = (x + X - 1) % X, (x + 1) % X, (x + 2) % X
    around = [xo, xr, xl]

    def ypeer(d):
        return (y + d) % Y

    def zpeer(d):
        return (z + d) % Z

    yorder = [2, 1, 3]
    zorder = [8, 7, 9, 6, 10, 5, 11, 4, 12, 3, 13, 2, 14, 1, 15]

    def columns(n):
        return pl.ds(pl.multiple_of(n * CHIP + core * FF, FF), FF)

    places = [(wg_hbm, wgu, 0), (wu_hbm, wgu, 1), (wd_hbm, wd, 0)]
    weights = [
        pltpu.make_async_copy(src.at[:, core], dst.at[:, :, columns(n)], w_sem.at[i])
        for i, (src, dst, n) in enumerate(places)
    ]

    bar = pltpu.get_barrier_semaphore()

    def greet(ee, ww):
        pl.semaphore_signal(bar, inc=1, device_id=(ee, ww), device_id_type=MESH)

    for d in zorder:
        greet(y * Z + zpeer(d), w)
    for d in yorder:
        greet(ypeer(d) * Z + z, w)
    for xx in around:
        greet(e, xx * 2 + core)
    greet(e, partner)
    for copy in weights:
        copy.start()

    def remote(src, dst, ssem, rsem, ee, ww):
        pltpu.make_async_remote_copy(
            src_ref=src, dst_ref=dst, send_sem=ssem, recv_sem=rsem,
            device_id=(ee, ww), device_id_type=MESH,
        ).start()

    row = iota((SLOTS, TOK), 0)
    expert = shr(row, 1)
    match = jnp.zeros((SLOTS, TOK), F32)
    weight = jnp.zeros((SLOTS, TOK), F32)
    for k in range(ids.shape[0]):
        hit = ids[k : k + 1, :] == expert
        match = jnp.where(hit, 1.0, match)
        weight = jnp.where(hit, rw[k : k + 1, :], weight)
    earlier = jnp.where(iota((TOK, TOK), 0) < iota((TOK, TOK), 1), 1.0, 0.0).astype(BF16)
    rank = dot(match.astype(BF16), earlier)
    chosen = [jnp.where(rank == float(q), match, 0.0) for q in range(Q)]
    half = [(row & 1) == h for h in range(2)]
    for q in range(Q):
        rows = sum(
            dot(jnp.where(half[h], chosen[q], 0.0).astype(BF16), tok[:, h * FH : (h + 1) * FH]) for h in range(2)
        ).astype(BF16)
        for f in range(NF):
            ysend[q, f] = rows[:, f * F : (f + 1) * F].reshape(Y, Z * 2, F)

    def order(a, b):
        return lax.shift_left(a & 3, 5) + lax.shift_left(shr(a, 3), 1) + (shr(a, 2) & 1) == b

    i0, i1 = iota((SLOTS, SLOTS), 0), iota((SLOTS, SLOTS), 1)
    to_z = jnp.where(order(i0, i1), 1.0, 0.0).astype(BF16)
    to_y = jnp.where(order(i1, i0), 1.0, 0.0).astype(BF16)
    first = (shr(iota((SLOTS, F), 0), 2) & 1) == 0

    pl.semaphore_wait(bar, len(zorder) + len(yorder) + len(around) + 1)

    def out_y(q, f):
        for d in yorder:
            remote(ysend.at[q, f, ypeer(d)], yrecv.at[q, f, y], y_ssem, y_rsem.at[q, f], ypeer(d) * Z + z, w)
        pltpu.make_async_copy(ysend.at[q, f, y], yrecv.at[q, f, y], y_rsem.at[q, f]).start()

    def trade_weights(q, f):
        for i, (src, dst, n) in enumerate(places):
            remote(src.at[:, 1 - core], dst.at[:, :, columns(n)], w_ssem.at[i], w_rsem.at[i], e, partner)

    def out_z(q, f):
        wait_bytes(yrecv.at[q, f], y_rsem.at[q, f])
        zsend[q, f] = dot(to_z, yrecv[q, f].reshape(SLOTS, F)).astype(BF16).reshape(Z, Y * 2, F)
        for d in zorder:
            remote(
                zsend.at[q, f, zpeer(d)], xall.at[q, f, x, z], z_ssem, z_rsem.at[q, f], y * Z + zpeer(d), w
            )
        pltpu.make_async_copy(zsend.at[q, f, z], xall.at[q, f, x, z], z_rsem.at[q, f]).start()

    def project(q, f, xx):
        block = xall[q, f, xx].reshape(SLOTS, F)
        low = jnp.where(first, block, jnp.zeros_like(block))
        high = jnp.where(first, jnp.zeros_like(block), block)
        return dot(low, wgu[xx, f * F : (f + 1) * F]) + dot(high, wgu[xx, FH + f * F : FH + (f + 1) * F])

    def out_x(q, f):
        wait_bytes(xall.at[q, f, x], z_rsem.at[q, f])
        for i, xx in enumerate(around):
            ref = xall.at[q, f, x]
            remote(ref, ref, x_ssem, x_rsem.at[q, f, i], e, xx * 2 + core)

    def weights_here(q, f):
        for copy in weights:
            copy.wait()
        for i, (src, dst, n) in enumerate(places):
            ref = dst.at[:, :, pl.ds(0, FF)]
            wait_bytes(ref, w_rsem.at[i])

    def gathered(q, f):
        total = project(q, f, x)
        for i, xx in ((1, xl), (2, xr), (0, xo)):
            wait_bytes(xall.at[q, f, xx], x_rsem.at[q, f, i])
            total = total + project(q, f, xx)
        if f > 0:
            total = total + part[q]
        part[q] = total
        if f == NF - 1:
            remote(part.at[q], other.at[q], p_ssem, p_rsem.at[q], e, partner)

    hidden = {}

    def activate(q, f):
        wait_bytes(other.at[q], p_rsem.at[q])
        total = part[q] + other[q]
        total = total.reshape(Z, Y * 2, 2 * CHIP)
        total = (total + pltpu.roll(total, Y, 1)).reshape(SLOTS, 2 * CHIP)
        gate, up = total[:, :CHIP], total[:, CHIP:]
        hidden[q] = (gate / (1.0 + jnp.exp(-gate)) * up).astype(BF16)

    def down(q, f, xx):
        low = dot(hidden[q], wd[xx, f * F : (f + 1) * F], ((1,), (1,)))
        high = dot(hidden[q], wd[xx, FH + f * F : FH + (f + 1) * F], ((1,), (1,)))
        return jnp.where(first, low, high)

    def back_x(q, f):
        for i, xx in enumerate(around):
            rsend[q, f, i] = down(q, f, xx).astype(BF16)
            remote(rsend.at[q, f, i], rrecv.at[q, f, i], r_ssem, r_rsem.at[q, f, i], e, xx * 2 + core)
        mine[q, f] = down(q, f, x)

    def back_z(q, f):
        total = mine[q, f]
        for i in (1, 2, 0):
            wait_bytes(rrecv.at[q, f, i], r_rsem.at[q, f, i])
            total = total + rrecv[q, f, i].astype(F32)
        zsend2[q, f] = total.astype(BF16).reshape(Z, Y * 2, F)
        for d in zorder:
            remote(
                zsend2.at[q, f, zpeer(d)], zrecv2.at[q, f, z], z2_ssem, z2_rsem.at[q, f], y * Z + zpeer(d), w
            )
        pltpu.make_async_copy(zsend2.at[q, f, z], zrecv2.at[q, f, z], z2_rsem.at[q, f]).start()

    def back_y(q, f):
        wait_bytes(zrecv2.at[q, f], z2_rsem.at[q, f])
        rows = dot(to_y, zrecv2[q, f].reshape(SLOTS, F)).astype(BF16)
        ysend2[q, f] = rows.reshape(Y, Z * 2, F)
        for d in yorder:
            remote(
                ysend2.at[q, f, ypeer(d)], yrecv2.at[q, f, y], y2_ssem, y2_rsem.at[q, f], ypeer(d) * Z + z, w
            )
        pltpu.make_async_copy(ysend2.at[q, f, y], yrecv2.at[q, f, y], y2_rsem.at[q, f]).start()

    def combine(q, f):
        wait_bytes(yrecv2.at[q, f], y2_rsem.at[q, f])
        returned = yrecv2[q, f].reshape(SLOTS, F)
        for h in range(2):
            coeff = jnp.where(half[h], weight * chosen[q], 0.0)
            high = coeff.astype(BF16)
            low = (coeff - high.astype(F32)).astype(BF16)
            total = dot(high, returned, ((0,), (0,))) + dot(low, returned, ((0,), (0,)))
            place = slice(h * FH + f * F, h * FH + (f + 1) * F)
            if q > 0:
                total = total + mixed[:, place]
            if q < Q - 1:
                mixed[:, place] = total
            else:
                out[:, place] = total.astype(BF16)

    gap = 3.5 / NF
    ready = 19.0 + gap * (NF - 1)
    steps = [
        (out_y, 0.0, 0.1, NF), (trade_weights, 0.3, 0, 0), (out_z, 2.6, 0.5, NF), (out_x, 9.0, gap, NF),
        (weights_here, 9.1, 0, 0), (gathered, 16.0, gap, NF), (activate, ready, gap * NF, 1),
        (back_x, ready + 0.1, gap, NF), (back_z, ready + 7.0, gap, NF), (back_y, ready + 13.0, gap, NF),
        (combine, ready + 16.0, gap, NF),
    ]
    plan = []
    for s, (step, at, later, each) in enumerate(steps):
        for q in range(Q if each else 1):
            for f in range(each or 1):
                plan.append((at + later * (q * each + f), s, q, f))
    for _, s, q, f in sorted(plan):
        steps[s][0](q, f)

    for i, (src, dst, n) in enumerate(places):
        wait_bytes(src.at[:, 1 - core], w_ssem.at[i])
    wait_bytes(ysend.at[:, :, pl.ds(0, Y - 1)], y_ssem)
    wait_bytes(zsend.at[:, :, pl.ds(0, Z - 1)], z_ssem)
    wait_bytes(xall.at[:, :, pl.ds(0, X - 1)], x_ssem)
    wait_bytes(part, p_ssem)
    wait_bytes(rsend, r_ssem)
    wait_bytes(zsend2.at[:, :, pl.ds(0, Z - 1)], z2_ssem)
    wait_bytes(ysend2.at[:, :, pl.ds(0, Y - 1)], y2_ssem)


def body(tokens, expert_ids, route_weight, gate_weight, up_weight, down_weight):
    vmem = pl.BlockSpec(memory_space=pltpu.VMEM)
    hbm = pl.BlockSpec(memory_space=pl.ANY)
    dma = pltpu.SemaphoreType.DMA
    ystage, zstage = pltpu.VMEM((Q, NF, Y, Z * 2, F), BF16), pltpu.VMEM((Q, NF, Z, Y * 2, F), BF16)
    return pl.pallas_call(
        kernel,
        out_shape=jax.ShapeDtypeStruct((TOK, FEAT), BF16),
        in_specs=[vmem, vmem, vmem, hbm, hbm, hbm],
        out_specs=vmem,
        scratch_shapes=[
            pltpu.VMEM((X, FEAT, 2 * CHIP), BF16),
            pltpu.VMEM((X, FEAT, CHIP), BF16),
            ystage, ystage, zstage,
            pltpu.VMEM((Q, NF, X, Z, Y * 2, F), BF16),
            pltpu.VMEM((Q, SLOTS, 2 * CHIP), F32),
            pltpu.VMEM((Q, SLOTS, 2 * CHIP), F32),
            pltpu.VMEM((Q, NF, X - 1, SLOTS, F), BF16),
            pltpu.VMEM((Q, NF, X - 1, SLOTS, F), BF16),
            pltpu.VMEM((Q, NF, SLOTS, F), F32),
            zstage, zstage, ystage, ystage,
            pltpu.VMEM((TOK, FEAT), F32),
            dma((3,)), dma((3,)), dma((3,)),
            dma, dma((Q, NF)), dma, dma((Q, NF)), dma, dma((Q, NF, X - 1)), dma, dma((Q,)),
            dma, dma((Q, NF, X - 1)), dma, dma((Q, NF)), dma, dma((Q, NF)),
        ],
        compiler_params=pltpu.CompilerParams(
            collective_id=0, has_side_effects=True, vmem_limit_bytes=60 * 2**20
        ),
        cost_estimate=pl.CostEstimate(
            flops=12 * SLOTS * X * 2 * FEAT * FF, bytes_accessed=12 * X * FEAT * FF, transcendentals=SLOTS * CHIP
        ),
        name="experts",
    )(
        tokens, expert_ids.T, route_weight.T,
        *(a.reshape(X, 2, FEAT, FF) for a in (gate_weight, up_weight, down_weight)),
    )


def solution(mesh):
    in_specs = (
        P("expert", "width"),
        P("expert", None),
        P("expert", None),
        P("expert", None, "width"),
        P("expert", None, "width"),
        P("expert", None, "width"),
    )
    out_specs = P("expert", "width")
    return jax.shard_map(body, mesh=mesh, in_specs=in_specs, out_specs=out_specs, check_vma=False)
```

```python
import jax
import jax.numpy as jnp
from jax import lax
from jax.experimental import pallas as pl
from jax.experimental.pallas import tpu as pltpu
from jax.sharding import PartitionSpec as P

MESH = pl.DeviceIdType.MESH
BF16 = jnp.bfloat16
F32 = jnp.float32
Y, Z, X = 4, 16, 4
TOK, FEAT, FF = 64, 768, 128
CHIP = 2 * FF
Q = 2
TW = 0.3
NF = 1
FH = FEAT // 2
F = FH // NF
LANES = 128
TILES = FEAT // LANES
SLOTS = Y * Z * 2


def dot(a, b, dims=((1,), (0,))):
    return lax.dot_general(a, b, (dims, ((), ())), preferred_element_type=F32)


def iota(shape, dim):
    return lax.broadcasted_iota(jnp.int32, shape, dim)


def shr(a, n):
    return lax.shift_right_logical(a, n)


def wait_bytes(ref, sem):
    pltpu.make_async_copy(ref, ref, sem).wait()


def kernel(
    tok, ids, rw, wg_hbm, wu_hbm, wd_hbm, out,
    wgu, wd, ysend, yrecv, zsend, xall, part, other, rsend, rrecv, mine,
    rows_zh, rows_ej, dsend, drecv, mixed,
    w_sem, w_ssem, w_rsem, y_ssem, y_rsem, z_ssem, z_rsem, x_ssem, x_rsem, p_ssem, p_rsem,
    r_ssem, r_rsem, d_ssem, d_rsem,
):
    e, w = lax.axis_index("expert"), lax.axis_index("width")
    y, z = e // Z, e % Z
    x, core = w // 2, w % 2
    partner = x * 2 + (1 - core)
    xl, xr, xo = (x + X - 1) % X, (x + 1) % X, (x + 2) % X
    around = [xo, xr, xl]

    def ypeer(d):
        return (y + d) % Y

    def zpeer(d):
        return (z + d) % Z

    yorder = [2, 1, 3]
    zorder = [8, 7, 9, 6, 10, 5, 11, 4, 12, 3, 13, 2, 14, 1, 15]

    def columns(n):
        return pl.ds(pl.multiple_of(n * CHIP + core * FF, FF), FF)

    places = [(wg_hbm, wgu, 0), (wu_hbm, wgu, 1), (wd_hbm, wd, 0)]
    weights = [
        pltpu.make_async_copy(src.at[:, core], dst.at[:, :, columns(n)], w_sem.at[i])
        for i, (src, dst, n) in enumerate(places)
    ]

    bar = pltpu.get_barrier_semaphore()

    def greet(ee, ww):
        pl.semaphore_signal(bar, inc=1, device_id=(ee, ww), device_id_type=MESH)

    for d in zorder:
        greet(y * Z + zpeer(d), w)
    for d in yorder:
        greet(ypeer(d) * Z + z, w)
    for xx in around:
        greet(e, xx * 2 + core)
    greet(e, partner)
    def remote(src, dst, ssem, rsem, ee, ww):
        pltpu.make_async_remote_copy(
            src_ref=src, dst_ref=dst, send_sem=ssem, recv_sem=rsem,
            device_id=(ee, ww), device_id_type=MESH,
        ).start()

    earlier = jnp.where(iota((TOK, TOK), 0) < iota((TOK, TOK), 1), 1.0, 0.0).astype(BF16)

    def routed(expert):
        match = jnp.zeros(expert.shape, F32)
        weight = jnp.zeros(expert.shape, F32)
        for k in range(ids.shape[0]):
            hit = ids[k : k + 1, :] == expert
            match = jnp.where(hit, 1.0, match)
            weight = jnp.where(hit, rw[k : k + 1, :], weight)
        rank = dot(match.astype(BF16), earlier)
        return [jnp.where(rank == float(q), match, 0.0) for q in range(Q)], weight

    row = iota((SLOTS, TOK), 0)
    chosen, _ = routed(shr(row, 1))
    half = [(row & 1) == h for h in range(2)]
    for q in range(Q):
        rows = sum(
            dot(jnp.where(half[h], chosen[q], 0.0).astype(BF16), tok[:, h * FH : (h + 1) * FH]) for h in range(2)
        ).astype(BF16)
        for f in range(NF):
            ysend[q, f] = rows[:, f * F : (f + 1) * F].reshape(Y, Z * 2, F)

    coeffs = []
    ones, weight = routed(iota((Y * Z, TOK), 0))
    for q in range(Q):
        high = (weight * ones[q]).astype(BF16)
        coeffs.append((high, (weight * ones[q] - high.astype(F32)).astype(BF16)))

    def order(a, b):
        return lax.shift_left(a & 3, 5) + lax.shift_left(shr(a, 3), 1) + (shr(a, 2) & 1) == b

    i0, i1 = iota((SLOTS, SLOTS), 0), iota((SLOTS, SLOTS), 1)
    to_z = jnp.where(order(i0, i1), 1.0, 0.0).astype(BF16)
    first = (shr(iota((SLOTS, F), 0), 2) & 1) == 0

    pl.semaphore_wait(bar, len(zorder) + len(yorder) + len(around) + 1)

    def out_y(q, f):
        for d in yorder:
            remote(ysend.at[q, f, ypeer(d)], yrecv.at[q, f, y], y_ssem, y_rsem.at[q, f], ypeer(d) * Z + z, w)
        pltpu.make_async_copy(ysend.at[q, f, y], yrecv.at[q, f, y], y_rsem.at[q, f]).start()

    def trade_weights(q, f):
        for copy in weights:
            copy.start()
        for i, (src, dst, n) in enumerate(places):
            remote(src.at[:, 1 - core], dst.at[:, :, columns(n)], w_ssem.at[i], w_rsem.at[i], e, partner)

    def out_z(q, f):
        wait_bytes(yrecv.at[q, f], y_rsem.at[q, f])
        zsend[q, f] = dot(to_z, yrecv[q, f].reshape(SLOTS, F)).astype(BF16).reshape(Z, Y * 2, F)
        for d in zorder:
            remote(
                zsend.at[q, f, zpeer(d)], xall.at[q, f, x, z], z_ssem, z_rsem.at[q, f], y * Z + zpeer(d), w
            )
        pltpu.make_async_copy(zsend.at[q, f, z], xall.at[q, f, x, z], z_rsem.at[q, f]).start()

    def project(q, f, xx):
        block = xall[q, f, xx].reshape(SLOTS, F)
        low = jnp.where(first, block, jnp.zeros_like(block))
        high = jnp.where(first, jnp.zeros_like(block), block)
        return dot(low, wgu[xx, f * F : (f + 1) * F]) + dot(high, wgu[xx, FH + f * F : FH + (f + 1) * F])

    def out_x(q, f):
        wait_bytes(xall.at[q, f, x], z_rsem.at[q, f])
        for i, xx in enumerate(around):
            ref = xall.at[q, f, x]
            remote(ref, ref, x_ssem, x_rsem.at[q, f, i], e, xx * 2 + core)

    def weights_here(q, f):
        for copy in weights:
            copy.wait()
        for i, (src, dst, n) in enumerate(places):
            ref = dst.at[:, :, pl.ds(0, FF)]
            wait_bytes(ref, w_rsem.at[i])

    def gathered(q, f):
        total = project(q, f, x)
        for i, xx in ((1, xl), (2, xr), (0, xo)):
            wait_bytes(xall.at[q, f, xx], x_rsem.at[q, f, i])
            total = total + project(q, f, xx)
        if f > 0:
            total = total + part[q]
        part[q] = total
        if f == NF - 1:
            remote(part.at[q], other.at[q], p_ssem, p_rsem.at[q], e, partner)

    hidden = {}

    def activate(q, f):
        wait_bytes(other.at[q], p_rsem.at[q])
        total = part[q] + other[q]
        total = total.reshape(Z, Y * 2, 2 * CHIP)
        total = (total + pltpu.roll(total, Y, 1)).reshape(SLOTS, 2 * CHIP)
        gate, up = total[:, :CHIP], total[:, CHIP:]
        hidden[q] = (gate / (1.0 + jnp.exp(-gate)) * up).astype(BF16)

    def down(q, f, xx):
        low = dot(hidden[q], wd[xx, f * F : (f + 1) * F], ((1,), (1,)))
        high = dot(hidden[q], wd[xx, FH + f * F : FH + (f + 1) * F], ((1,), (1,)))
        return jnp.where(first, low, high)

    def back_x(q, f):
        for i, xx in enumerate(around):
            rsend[q, f, i] = down(q, f, xx).astype(BF16)
            remote(rsend.at[q, f, i], rrecv.at[q, f, i], r_ssem, r_rsem.at[q, f, i], e, xx * 2 + core)
        mine[q, f] = down(q, f, x)

    def back(q, f):
        total = mine[q, f]
        for i in (1, 2, 0):
            wait_bytes(rrecv.at[q, f, i], r_rsem.at[q, f, i])
            total = total + rrecv[q, f, i].astype(F32)
        for c in range(TILES // 2):
            rows_zh[pl.ds(c * SLOTS, SLOTS), :] = total[:, c * LANES : (c + 1) * LANES]
        for h in range(2):
            for yy in range(Y):
                for c in range(TILES // 2):
                    rows_ej[pl.ds(yy * Z * TILES + h * TILES // 2 + c, Z, TILES), :] = rows_zh[
                        pl.ds(c * SLOTS + h * Y + yy, Z, 2 * Y), :
                    ]
        dsend[q] = rows_ej[...].astype(BF16).reshape(Y * Z, TILES // 2, 2, LANES)
        for d in zorder + [0]:
            for dy in yorder + [0]:
                if d or dy:
                    peer = ypeer(dy) * Z + zpeer(d)
                    remote(dsend.at[q, peer], drecv.at[q, e], d_ssem, d_rsem.at[q], peer, w)
        pltpu.make_async_copy(dsend.at[q, e], drecv.at[q, e], d_rsem.at[q]).start()

    def combine(q, f):
        wait_bytes(drecv.at[q], d_rsem.at[q])
        rows_ej[...] = drecv[q].astype(F32).reshape(Y * Z * TILES, LANES)
        returned = jnp.concatenate(
            [rows_ej[pl.ds(j, Y * Z, TILES), :].astype(BF16) for j in range(TILES)], axis=1
        )
        total = sum(dot(c, returned, ((0,), (0,))) for c in coeffs[q])
        if q > 0:
            total = total + mixed[...]
        if q < Q - 1:
            mixed[...] = total
        else:
            out[...] = total.astype(BF16)

    gap = 3.5 / NF
    ready = 19.0 + gap * (NF - 1)
    steps = [
        (out_y, 0.0, 0.1, NF), (trade_weights, TW, 0, 0), (out_z, 2.6, 0.5, NF), (out_x, 9.0, gap, NF),
        (weights_here, 9.1, 0, 0), (gathered, 16.0, gap, NF), (activate, ready, gap * NF, 1),
        (back_x, ready + 0.1, gap, NF), (back, ready + 7.0, gap, NF), (combine, ready + 15.0, gap, NF),
    ]
    plan = []
    for s, (step, at, later, each) in enumerate(steps):
        for q in range(Q if each else 1):
            for f in range(each or 1):
                plan.append((at + later * (q * each + f), s, q, f))
    for _, s, q, f in sorted(plan):
        steps[s][0](q, f)

    for i, (src, dst, n) in enumerate(places):
        wait_bytes(src.at[:, 1 - core], w_ssem.at[i])
    wait_bytes(ysend.at[:, :, pl.ds(0, Y - 1)], y_ssem)
    wait_bytes(zsend.at[:, :, pl.ds(0, Z - 1)], z_ssem)
    wait_bytes(xall.at[:, :, pl.ds(0, X - 1)], x_ssem)
    wait_bytes(part, p_ssem)
    wait_bytes(rsend, r_ssem)
    wait_bytes(dsend.at[:, pl.ds(0, Y * Z - 1)], d_ssem)


def body(tokens, expert_ids, route_weight, gate_weight, up_weight, down_weight):
    vmem = pl.BlockSpec(memory_space=pltpu.VMEM)
    hbm = pl.BlockSpec(memory_space=pl.ANY)
    dma = pltpu.SemaphoreType.DMA
    ystage, zstage = pltpu.VMEM((Q, NF, Y, Z * 2, F), BF16), pltpu.VMEM((Q, NF, Z, Y * 2, F), BF16)
    return pl.pallas_call(
        kernel,
        out_shape=jax.ShapeDtypeStruct((TOK, FEAT), BF16),
        in_specs=[vmem, vmem, vmem, hbm, hbm, hbm],
        out_specs=vmem,
        scratch_shapes=[
            pltpu.VMEM((X, FEAT, 2 * CHIP), BF16),
            pltpu.VMEM((X, FEAT, CHIP), BF16),
            ystage, ystage, zstage,
            pltpu.VMEM((Q, NF, X, Z, Y * 2, F), BF16),
            pltpu.VMEM((Q, SLOTS, 2 * CHIP), F32),
            pltpu.VMEM((Q, SLOTS, 2 * CHIP), F32),
            pltpu.VMEM((Q, NF, X - 1, SLOTS, F), BF16),
            pltpu.VMEM((Q, NF, X - 1, SLOTS, F), BF16),
            pltpu.VMEM((Q, NF, SLOTS, F), F32),
            pltpu.VMEM((TILES // 2 * SLOTS, LANES), F32),
            pltpu.VMEM((Y * Z * TILES, LANES), F32),
            pltpu.VMEM((Q, Y * Z, TILES // 2, 2, LANES), BF16),
            pltpu.VMEM((Q, Y * Z, TILES // 2, 2, LANES), BF16),
            pltpu.VMEM((TOK, FEAT), F32),
            dma((3,)), dma((3,)), dma((3,)),
            dma, dma((Q, NF)), dma, dma((Q, NF)), dma, dma((Q, NF, X - 1)), dma, dma((Q,)),
            dma, dma((Q, NF, X - 1)), dma, dma((Q,)),
        ],
        compiler_params=pltpu.CompilerParams(
            collective_id=0, has_side_effects=True, vmem_limit_bytes=60 * 2**20
        ),
        cost_estimate=pl.CostEstimate(
            flops=12 * SLOTS * X * 2 * FEAT * FF, bytes_accessed=12 * X * FEAT * FF, transcendentals=SLOTS * CHIP
        ),
        name="experts",
    )(
        tokens, expert_ids.T, route_weight.T,
        *(a.reshape(X, 2, FEAT, FF) for a in (gate_weight, up_weight, down_weight)),
    )


def solution(mesh):
    in_specs = (
        P("expert", "width"),
        P("expert", None),
        P("expert", None),
        P("expert", None, "width"),
        P("expert", None, "width"),
        P("expert", None, "width"),
    )
    out_specs = P("expert", "width")
    return jax.shard_map(body, mesh=mesh, in_specs=in_specs, out_specs=out_specs, check_vma=False)
```

```python
import jax
import jax.numpy as jnp
from jax import lax
from jax.experimental import pallas as pl
from jax.experimental.pallas import tpu as pltpu
from jax.sharding import PartitionSpec as P

MESH = pl.DeviceIdType.MESH
BF16 = jnp.bfloat16
F32 = jnp.float32
Y, Z, X = 4, 16, 4
TOK, FEAT, FF = 64, 768, 128
CHIP = 2 * FF
Q = 2
ALL = Y * Z
K = Q * 2
ROWS = ALL // 2
LANES = 128
TILES = FEAT // LANES


def dot(a, b, dims=((1,), (0,))):
    return lax.dot_general(a, b, (dims, ((), ())), preferred_element_type=F32)


def iota(shape, dim):
    return lax.broadcasted_iota(jnp.int32, shape, dim)


def wait_bytes(ref, sem):
    pltpu.make_async_copy(ref, ref, sem).wait()


def kernel(
    tok, ids, rw, wg_hbm, wu_hbm, wd_hbm, out,
    wgu, wd, flat, osend, orecv, xall, part, other, rsend, rrecv, mine, dsend, drecv, mixed,
    w_sem, w_ssem, w_rsem, column_sem, o_ssem, o_rsem, x_ssem, x_rsem, p_ssem, p_rsem,
    r_ssem, r_rsem, d_ssem, d_rsem,
):
    e, w = lax.axis_index("expert"), lax.axis_index("width")
    y, z = e // Z, e % Z
    x, core = w // 2, w % 2
    partner = x * 2 + (1 - core)
    xl, xr, xo = (x + X - 1) % X, (x + 1) % X, (x + 2) % X
    around = [xo, xr, xl]
    yorder = [2, 1, 3]
    zorder = [8, 7, 9, 6, 10, 5, 11, 4, 12, 3, 13, 2, 14, 1, 15]

    def peer(dy, dz):
        return (y + dy) % Y * Z + (z + dz) % Z

    near = [(0, dz) for dz in zorder] + [(dy, 0) for dy in yorder]
    far = [(dy, dz) for dz in zorder for dy in yorder]

    def place(ee):
        return ee // 2

    def parity(peers, p):
        return [(dy, dz) for dy, dz in peers if dz % 2 == p]

    def columns(n):
        return pl.ds(pl.multiple_of(n * CHIP + core * FF, FF), FF)

    places = [(wg_hbm, wgu, 0), (wu_hbm, wgu, 1), (wd_hbm, wd, 0)]
    weights = [
        pltpu.make_async_copy(src.at[:, core], dst.at[:, :, columns(n)], w_sem.at[i])
        for i, (src, dst, n) in enumerate(places)
    ]

    bar = pltpu.get_barrier_semaphore()

    def greet(ee, ww):
        pl.semaphore_signal(bar, inc=1, device_id=(ee, ww), device_id_type=MESH)

    for dy, dz in near:
        greet(peer(dy, dz), w)
    for xx in around:
        greet(e, xx * 2 + core)
    greet(e, partner)

    def remote(src, dst, ssem, rsem, ee, ww):
        pltpu.make_async_remote_copy(
            src_ref=src, dst_ref=dst, send_sem=ssem, recv_sem=rsem,
            device_id=(ee, ww), device_id_type=MESH,
        ).start()

    def fold(rows):
        n = rows.shape[0]
        for j in range(TILES):
            flat[pl.ds(j, n, TILES), :] = rows[:, j * LANES : (j + 1) * LANES]
        return flat[pl.ds(0, n * TILES), :].astype(BF16).reshape(n, TILES // 2, 2, LANES)

    def unfold(rows):
        n = rows.shape[0]
        flat[pl.ds(0, n * TILES), :] = rows.astype(F32).reshape(n * TILES, LANES)
        return jnp.concatenate([flat[pl.ds(j, n, TILES), :].astype(BF16) for j in range(TILES)], axis=1)

    expert = iota((ALL, TOK), 0)
    match = jnp.zeros((ALL, TOK), F32)
    weight = jnp.zeros((ALL, TOK), F32)
    for k in range(ids.shape[0]):
        hit = ids[k : k + 1, :] == expert
        match = jnp.where(hit, 1.0, match)
        weight = jnp.where(hit, rw[k : k + 1, :], weight)
    earlier = jnp.where(iota((TOK, TOK), 0) < iota((TOK, TOK), 1), 1.0, 0.0).astype(BF16)
    rank = dot(match.astype(BF16), earlier)
    coeffs = []
    for q in range(Q):
        chosen = jnp.where(rank == float(q), match, 0.0)
        high = (weight * chosen).astype(BF16)
        coeffs.append((high, (weight * chosen - high.astype(F32)).astype(BF16)))
        osend[q] = fold(dot(chosen.astype(BF16), tok[...]))

    pl.semaphore_wait(bar, len(near) + len(around) + 1)

    def column_is_in():
        for dy in yorder:
            pl.semaphore_signal(column_sem, inc=1, device_id=(peer(dy, 0), w), device_id_type=MESH)

    def columns_are_in():
        pl.semaphore_wait(column_sem, len(yorder))

    def out_to(k, peers):
        q, p = k // 2, k % 2
        for dy, dz in parity(peers, p):
            remote(
                osend.at[q, peer(dy, dz)], orecv.at[k, place(e)], o_ssem, o_rsem.at[k], peer(dy, dz), w
            )

    def out_own(q):
        pltpu.make_async_copy(osend.at[q, e], orecv.at[q * 2, place(e)], o_rsem.at[q * 2]).start()

    def start_weights():
        for copy in weights:
            copy.start()
        for i, (src, dst, n) in enumerate(places):
            remote(src.at[:, 1 - core], dst.at[:, :, columns(n)], w_ssem.at[i], w_rsem.at[i], e, partner)

    def weights_here():
        for copy in weights:
            copy.wait()
        for i, (src, dst, n) in enumerate(places):
            wait_bytes(dst.at[:, :, pl.ds(0, FF)], w_rsem.at[i])

    def out_x(k):
        wait_bytes(orecv.at[k], o_rsem.at[k])
        xall[k, x] = unfold(orecv[k])
        ref = xall.at[k, x]
        for i, xx in enumerate(around):
            remote(ref, ref, x_ssem, x_rsem.at[k, i], e, xx * 2 + core)

    def project(k, xx):
        return dot(xall[k, xx], wgu[xx])

    def gathered(k):
        total = project(k, x)
        for i, xx in ((1, xl), (2, xr), (0, xo)):
            wait_bytes(xall.at[k, xx], x_rsem.at[k, i])
            total = total + project(k, xx)
        part[k] = total
        remote(part.at[k], other.at[k], p_ssem, p_rsem.at[k], e, partner)

    def back_x(k):
        wait_bytes(other.at[k], p_rsem.at[k])
        total = part[k] + other[k]
        gate, up = total[:, :CHIP], total[:, CHIP:]
        hidden = (gate / (1.0 + jnp.exp(-gate)) * up).astype(BF16)
        for i, xx in enumerate(around):
            rsend[k, i] = dot(hidden, wd[xx], ((1,), (1,))).astype(BF16)
            remote(rsend.at[k, i], rrecv.at[k, i], r_ssem, r_rsem.at[k, i], e, xx * 2 + core)
        mine[k] = dot(hidden, wd[x], ((1,), (1,)))

    def back(k):
        total = mine[k]
        for i in (1, 2, 0):
            wait_bytes(rrecv.at[k, i], r_rsem.at[k, i])
            total = total + rrecv[k, i].astype(F32)
        dsend[k] = fold(total)
        q, p = k // 2, k % 2
        for dy, dz in parity(far, p) + parity(near, p):
            to = peer(dy, dz)
            remote(dsend.at[k, place(to)], drecv.at[q, e], d_ssem, d_rsem.at[q], to, w)
        if p == 0:
            pltpu.make_async_copy(dsend.at[k, place(e)], drecv.at[q, e], d_rsem.at[q]).start()

    def combine(q):
        wait_bytes(drecv.at[q], d_rsem.at[q])
        returned = unfold(drecv[q])
        total = sum(dot(c, returned, ((0,), (0,))) for c in coeffs[q])
        if q > 0:
            total = total + mixed[...]
        if q < Q - 1:
            mixed[...] = total
        else:
            out[...] = total.astype(BF16)

    column_is_in()
    for k in range(K):
        out_to(k, near)
    columns_are_in()
    for k in range(K):
        out_to(k, far)
        if k % 2 == 0:
            out_own(k // 2)
    start_weights()
    for k in range(K):
        out_x(k)
    weights_here()
    gathered(0)
    for k in range(1, K):
        gathered(k)
        back_x(k - 1)
    back_x(K - 1)
    for k in range(K):
        back(k)
    for q in range(Q):
        combine(q)

    for i, (src, dst, n) in enumerate(places):
        wait_bytes(src.at[:, 1 - core], w_ssem.at[i])
    wait_bytes(osend.at[:, pl.ds(0, ALL - 1)], o_ssem)
    wait_bytes(xall.at[:, pl.ds(0, X - 1)], x_ssem)
    wait_bytes(part, p_ssem)
    wait_bytes(rsend, r_ssem)
    wait_bytes(drecv.at[:, pl.ds(0, ALL - 1)], d_ssem)


def body(tokens, expert_ids, route_weight, gate_weight, up_weight, down_weight):
    vmem = pl.BlockSpec(memory_space=pltpu.VMEM)
    hbm = pl.BlockSpec(memory_space=pl.ANY)
    dma = pltpu.SemaphoreType.DMA
    lying = (TILES // 2, 2, LANES)
    return pl.pallas_call(
        kernel,
        out_shape=jax.ShapeDtypeStruct((TOK, FEAT), BF16),
        in_specs=[vmem, vmem, vmem, hbm, hbm, hbm],
        out_specs=vmem,
        scratch_shapes=[
            pltpu.VMEM((X, FEAT, 2 * CHIP), BF16),
            pltpu.VMEM((X, FEAT, CHIP), BF16),
            pltpu.VMEM((ALL * TILES, LANES), F32),
            pltpu.VMEM((Q, ALL, *lying), BF16),
            pltpu.VMEM((K, ROWS, *lying), BF16),
            pltpu.VMEM((K, X, ROWS, FEAT), BF16),
            pltpu.VMEM((K, ROWS, 2 * CHIP), F32),
            pltpu.VMEM((K, ROWS, 2 * CHIP), F32),
            pltpu.VMEM((K, X - 1, ROWS, FEAT), BF16),
            pltpu.VMEM((K, X - 1, ROWS, FEAT), BF16),
            pltpu.VMEM((K, ROWS, FEAT), F32),
            pltpu.VMEM((K, ROWS, *lying), BF16),
            pltpu.VMEM((Q, ALL, *lying), BF16),
            pltpu.VMEM((TOK, FEAT), F32),
            dma((3,)), dma((3,)), dma((3,)), pltpu.SemaphoreType.REGULAR,
            dma, dma((K,)), dma, dma((K, X - 1)), dma, dma((K,)),
            dma, dma((K, X - 1)), dma, dma((Q,)),
        ],
        compiler_params=pltpu.CompilerParams(
            collective_id=0, has_side_effects=True, vmem_limit_bytes=60 * 2**20
        ),
        cost_estimate=pl.CostEstimate(
            flops=12 * ALL * X * 2 * FEAT * FF, bytes_accessed=12 * X * FEAT * FF, transcendentals=2 * ALL * CHIP
        ),
        name="experts",
    )(
        tokens, expert_ids.T, route_weight.T,
        *(a.reshape(X, 2, FEAT, FF) for a in (gate_weight, up_weight, down_weight)),
    )


def solution(mesh):
    in_specs = (
        P("expert", "width"),
        P("expert", None),
        P("expert", None),
        P("expert", None, "width"),
        P("expert", None, "width"),
        P("expert", None, "width"),
    )
    out_specs = P("expert", "width")
    return jax.shard_map(body, mesh=mesh, in_specs=in_specs, out_specs=out_specs, check_vma=False)
```

```python
import jax
import jax.numpy as jnp
from jax import lax
from jax.experimental import pallas as pl
from jax.experimental.pallas import tpu as pltpu
from jax.sharding import PartitionSpec as P

MESH = pl.DeviceIdType.MESH
BF16 = jnp.bfloat16
F32 = jnp.float32
Y, Z, X = 4, 16, 4
TOK, FEAT, FF = 64, 768, 128
CHIP = 2 * FF
Q = 2
ALL = Y * Z
K = Q * 2
ROWS = ALL // 2
LANES = 128
TILES = FEAT // LANES


def dot(a, b, dims=((1,), (0,))):
    return lax.dot_general(a, b, (dims, ((), ())), preferred_element_type=F32)


def iota(shape, dim):
    return lax.broadcasted_iota(jnp.int32, shape, dim)


def wait_bytes(ref, sem):
    pltpu.make_async_copy(ref, ref, sem).wait()


def kernel(
    tok_hbm, ids_hbm, rw_hbm, wg_hbm, wu_hbm, wd_hbm, out,
    tok, ids, rw, wgu, wd, flat, osend, orecv, xall, part, other, rsend, rrecv, mine, dsend, drecv, mixed,
    in_sem, w_sem, w_ssem, w_rsem, column_sem, o_ssem, o_rsem, x_ssem, x_rsem, p_ssem, p_rsem,
    r_ssem, r_rsem, d_ssem, d_rsem,
):
    inputs = [
        pltpu.make_async_copy(src, dst, in_sem.at[i])
        for i, (src, dst) in enumerate(((ids_hbm, ids), (rw_hbm, rw), (tok_hbm, tok)))
    ]
    for copy in inputs:
        copy.start()
    e, w = lax.axis_index("expert"), lax.axis_index("width")
    y, z = e // Z, e % Z
    x, core = w // 2, w % 2
    partner = x * 2 + (1 - core)
    xl, xr, xo = (x + X - 1) % X, (x + 1) % X, (x + 2) % X
    around = [xo, xr, xl]
    yorder = [2, 1, 3]
    zorder = [8, 7, 9, 6, 10, 5, 11, 4, 12, 3, 13, 2, 14, 1, 15]

    def peer(dy, dz):
        return (y + dy) % Y * Z + (z + dz) % Z

    near = [(0, dz) for dz in zorder] + [(dy, 0) for dy in yorder]
    far = [(dy, dz) for dz in zorder for dy in yorder]

    def place(ee):
        return ee // 2

    def parity(peers, p):
        return [(dy, dz) for dy, dz in peers if dz % 2 == p]

    def columns(n):
        return pl.ds(pl.multiple_of(n * CHIP + core * FF, FF), FF)

    places = [(wg_hbm, wgu, 0), (wu_hbm, wgu, 1), (wd_hbm, wd, 0)]
    weights = [
        pltpu.make_async_copy(src.at[:, core], dst.at[:, :, columns(n)], w_sem.at[i])
        for i, (src, dst, n) in enumerate(places)
    ]

    bar = pltpu.get_barrier_semaphore()

    def greet(ee, ww):
        pl.semaphore_signal(bar, inc=1, device_id=(ee, ww), device_id_type=MESH)

    for dy, dz in near:
        greet(peer(dy, dz), w)
    for xx in around:
        greet(e, xx * 2 + core)
    greet(e, partner)

    def remote(src, dst, ssem, rsem, ee, ww):
        pltpu.make_async_remote_copy(
            src_ref=src, dst_ref=dst, send_sem=ssem, recv_sem=rsem,
            device_id=(ee, ww), device_id_type=MESH,
        ).start()

    def fold(rows):
        n = rows.shape[0]
        for j in range(TILES):
            flat[pl.ds(j, n, TILES), :] = rows[:, j * LANES : (j + 1) * LANES]
        return flat[pl.ds(0, n * TILES), :].astype(BF16).reshape(n, TILES // 2, 2, LANES)

    def unfold(rows):
        n = rows.shape[0]
        flat[pl.ds(0, n * TILES), :] = rows.astype(F32).reshape(n * TILES, LANES)
        return jnp.concatenate([flat[pl.ds(j, n, TILES), :].astype(BF16) for j in range(TILES)], axis=1)

    for copy in inputs:
        copy.wait()
    expert = iota((ALL, TOK), 0)
    match = jnp.zeros((ALL, TOK), F32)
    weight = jnp.zeros((ALL, TOK), F32)
    for k in range(ids.shape[0]):
        hit = ids[k : k + 1, :] == expert
        match = jnp.where(hit, 1.0, match)
        weight = jnp.where(hit, rw[k : k + 1, :], weight)
    earlier = jnp.where(iota((TOK, TOK), 0) < iota((TOK, TOK), 1), 1.0, 0.0).astype(BF16)
    rank = dot(match.astype(BF16), earlier)
    chosen = [jnp.where(rank == float(q), match, 0.0) for q in range(Q)]
    osend[0] = fold(dot(chosen[0].astype(BF16), tok[...]))

    pl.semaphore_wait(bar, len(near) + len(around) + 1)

    def column_is_in():
        for dy in yorder:
            pl.semaphore_signal(column_sem, inc=1, device_id=(peer(dy, 0), w), device_id_type=MESH)

    def columns_are_in():
        pl.semaphore_wait(column_sem, len(yorder))

    def out_to(k, peers):
        q, p = k // 2, k % 2
        for dy, dz in parity(peers, p):
            remote(
                osend.at[q, peer(dy, dz)], orecv.at[k, place(e)], o_ssem, o_rsem.at[k], peer(dy, dz), w
            )

    def out_own(q):
        pltpu.make_async_copy(osend.at[q, e], orecv.at[q * 2, place(e)], o_rsem.at[q * 2]).start()

    def start_weights():
        for copy in weights:
            copy.start()
        for i, (src, dst, n) in enumerate(places):
            remote(src.at[:, 1 - core], dst.at[:, :, columns(n)], w_ssem.at[i], w_rsem.at[i], e, partner)

    def weights_here():
        for copy in weights:
            copy.wait()
        for i, (src, dst, n) in enumerate(places):
            wait_bytes(dst.at[:, :, pl.ds(0, FF)], w_rsem.at[i])

    def out_x(k):
        wait_bytes(orecv.at[k], o_rsem.at[k])
        xall[k, x] = unfold(orecv[k])
        ref = xall.at[k, x]
        for i, xx in enumerate(around):
            remote(ref, ref, x_ssem, x_rsem.at[k, i], e, xx * 2 + core)

    def project(k, xx):
        return dot(xall[k, xx], wgu[xx])

    def gathered(k):
        total = project(k, x)
        for i, xx in ((1, xl), (2, xr), (0, xo)):
            wait_bytes(xall.at[k, xx], x_rsem.at[k, i])
            total = total + project(k, xx)
        part[k] = total
        remote(part.at[k], other.at[k], p_ssem, p_rsem.at[k], e, partner)

    def back_x(k):
        wait_bytes(other.at[k], p_rsem.at[k])
        total = part[k] + other[k]
        gate, up = total[:, :CHIP], total[:, CHIP:]
        hidden = (gate / (1.0 + jnp.exp(-gate)) * up).astype(BF16)
        for i, xx in enumerate(around):
            rsend[k, i] = dot(hidden, wd[xx], ((1,), (1,))).astype(BF16)
            remote(rsend.at[k, i], rrecv.at[k, i], r_ssem, r_rsem.at[k, i], e, xx * 2 + core)
        mine[k] = dot(hidden, wd[x], ((1,), (1,)))

    def back(k):
        total = mine[k]
        for i in (1, 2, 0):
            wait_bytes(rrecv.at[k, i], r_rsem.at[k, i])
            total = total + rrecv[k, i].astype(F32)
        dsend[k] = fold(total)
        q, p = k // 2, k % 2
        for dy, dz in parity(far, p) + parity(near, p):
            to = peer(dy, dz)
            remote(dsend.at[k, place(to)], drecv.at[q, e], d_ssem, d_rsem.at[q], to, w)
        if p == 0:
            pltpu.make_async_copy(dsend.at[k, place(e)], drecv.at[q, e], d_rsem.at[q]).start()

    def combine(q):
        wait_bytes(drecv.at[q], d_rsem.at[q])
        returned = unfold(drecv[q])
        total = sum(dot(c, returned, ((0,), (0,))) for c in coeffs[q])
        if q > 0:
            total = total + mixed[...]
        if q < Q - 1:
            mixed[...] = total
        else:
            out[...] = total.astype(BF16)

    column_is_in()
    out_to(0, near)
    out_to(1, near)
    osend[1] = fold(dot(chosen[1].astype(BF16), tok[...]))
    out_to(2, near)
    out_to(3, near)
    columns_are_in()
    for k in range(K):
        out_to(k, far)
        if k % 2 == 0:
            out_own(k // 2)
    start_weights()
    coeffs = []
    for q in range(Q):
        high = (weight * chosen[q]).astype(BF16)
        coeffs.append((high, (weight * chosen[q] - high.astype(F32)).astype(BF16)))
    for k in range(K):
        out_x(k)
    weights_here()
    gathered(0)
    for k in range(1, K):
        gathered(k)
        back_x(k - 1)
    back_x(K - 1)
    for k in range(K):
        back(k)
    for q in range(Q):
        combine(q)

    for i, (src, dst, n) in enumerate(places):
        wait_bytes(src.at[:, 1 - core], w_ssem.at[i])
    wait_bytes(osend.at[:, pl.ds(0, ALL - 1)], o_ssem)
    wait_bytes(xall.at[:, pl.ds(0, X - 1)], x_ssem)
    wait_bytes(part, p_ssem)
    wait_bytes(rsend, r_ssem)
    wait_bytes(drecv.at[:, pl.ds(0, ALL - 1)], d_ssem)


def body(tokens, expert_ids, route_weight, gate_weight, up_weight, down_weight):
    vmem = pl.BlockSpec(memory_space=pltpu.VMEM)
    hbm = pl.BlockSpec(memory_space=pl.ANY)
    dma = pltpu.SemaphoreType.DMA
    lying = (TILES // 2, 2, LANES)
    return pl.pallas_call(
        kernel,
        out_shape=jax.ShapeDtypeStruct((TOK, FEAT), BF16),
        in_specs=[hbm] * 6,
        out_specs=vmem,
        scratch_shapes=[
            pltpu.VMEM((TOK, FEAT), BF16),
            pltpu.VMEM(expert_ids.T.shape, jnp.int32),
            pltpu.VMEM(route_weight.T.shape, F32),
            pltpu.VMEM((X, FEAT, 2 * CHIP), BF16),
            pltpu.VMEM((X, FEAT, CHIP), BF16),
            pltpu.VMEM((ALL * TILES, LANES), F32),
            pltpu.VMEM((Q, ALL, *lying), BF16),
            pltpu.VMEM((K, ROWS, *lying), BF16),
            pltpu.VMEM((K, X, ROWS, FEAT), BF16),
            pltpu.VMEM((K, ROWS, 2 * CHIP), F32),
            pltpu.VMEM((K, ROWS, 2 * CHIP), F32),
            pltpu.VMEM((K, X - 1, ROWS, FEAT), BF16),
            pltpu.VMEM((K, X - 1, ROWS, FEAT), BF16),
            pltpu.VMEM((K, ROWS, FEAT), F32),
            pltpu.VMEM((K, ROWS, *lying), BF16),
            pltpu.VMEM((Q, ALL, *lying), BF16),
            pltpu.VMEM((TOK, FEAT), F32),
            dma((3,)), dma((3,)), dma((3,)), dma((3,)), pltpu.SemaphoreType.REGULAR,
            dma, dma((K,)), dma, dma((K, X - 1)), dma, dma((K,)),
            dma, dma((K, X - 1)), dma, dma((Q,)),
        ],
        compiler_params=pltpu.CompilerParams(
            collective_id=0, has_side_effects=True, vmem_limit_bytes=60 * 2**20
        ),
        cost_estimate=pl.CostEstimate(
            flops=12 * ALL * X * 2 * FEAT * FF, bytes_accessed=12 * X * FEAT * FF, transcendentals=2 * ALL * CHIP
        ),
        name="experts",
    )(
        tokens, expert_ids.T, route_weight.T,
        *(a.reshape(X, 2, FEAT, FF) for a in (gate_weight, up_weight, down_weight)),
    )


def solution(mesh):
    in_specs = (
        P("expert", "width"),
        P("expert", None),
        P("expert", None),
        P("expert", None, "width"),
        P("expert", None, "width"),
        P("expert", None, "width"),
    )
    out_specs = P("expert", "width")
    return jax.shard_map(body, mesh=mesh, in_specs=in_specs, out_specs=out_specs, check_vma=False)
```

```python
import jax
import jax.numpy as jnp
from jax import lax
from jax.experimental import pallas as pl
from jax.experimental.pallas import tpu as pltpu
from jax.sharding import PartitionSpec as P

MESH = pl.DeviceIdType.MESH
BF16 = jnp.bfloat16
F32 = jnp.float32
Y, Z, X = 4, 16, 4
TOK, FEAT, FF = 64, 768, 128
CHIP = 2 * FF
Q = 2
ALL = Y * Z
K = Q * 2
ROWS = ALL // 2
LANES = 128
TILES = FEAT // LANES


def dot(a, b, dims=((1,), (0,))):
    return lax.dot_general(a, b, (dims, ((), ())), preferred_element_type=F32)


def iota(shape, dim):
    return lax.broadcasted_iota(jnp.int32, shape, dim)


def wait_bytes(ref, sem):
    pltpu.make_async_copy(ref, ref, sem).wait()


def kernel(
    tok_hbm, ids_hbm, rw_hbm, wg_hbm, wu_hbm, wd_hbm, out,
    tok, ids, rw, wgu, wd, flat, osend, orecv, xall, part, other, rsend, rrecv, mine, dsend, drecv, mixed,
    in_sem, w_sem, w_ssem, w_rsem, column_sem, o_ssem, o_rsem, x_ssem, x_rsem, p_ssem, p_rsem,
    r_ssem, r_rsem, d_ssem, d_rsem,
):
    inputs = [
        pltpu.make_async_copy(src, dst, in_sem.at[i])
        for i, (src, dst) in enumerate(((ids_hbm, ids), (rw_hbm, rw), (tok_hbm, tok)))
    ]
    for copy in inputs:
        copy.start()
    e, w = lax.axis_index("expert"), lax.axis_index("width")
    y, z = e // Z, e % Z
    x, core = w // 2, w % 2
    partner = x * 2 + (1 - core)
    xl, xr, xo = (x + X - 1) % X, (x + 1) % X, (x + 2) % X
    around = [xr, xl, xo]
    yorder = [2, 1, 3]
    zorder = [8, 7, 9, 6, 10, 5, 11, 4, 12, 3, 13, 2, 14, 1, 15]

    def peer(dy, dz):
        return (y + dy) % Y * Z + (z + dz) % Z

    near = [(0, dz) for dz in zorder] + [(dy, 0) for dy in yorder]
    far = [(dy, dz) for dz in zorder for dy in yorder]

    def place(ee):
        return ee // 2

    def parity(peers, p):
        return [(dy, dz) for dy, dz in peers if dz % 2 == p]

    def columns(n):
        return pl.ds(pl.multiple_of(n * CHIP + core * FF, FF), FF)

    places = [(wg_hbm, wgu, 0), (wu_hbm, wgu, 1), (wd_hbm, wd, 0)]
    weights = [
        pltpu.make_async_copy(src.at[:, core], dst.at[:, :, columns(n)], w_sem.at[i])
        for i, (src, dst, n) in enumerate(places)
    ]

    bar = pltpu.get_barrier_semaphore()

    def greet(ee, ww):
        pl.semaphore_signal(bar, inc=1, device_id=(ee, ww), device_id_type=MESH)

    for dy, dz in near:
        greet(peer(dy, dz), w)
    for xx in around:
        greet(e, xx * 2 + core)
    greet(e, partner)
    for dy, dz in far:
        greet(peer(dy, dz), w)

    def remote(src, dst, ssem, rsem, ee, ww):
        pltpu.make_async_remote_copy(
            src_ref=src, dst_ref=dst, send_sem=ssem, recv_sem=rsem,
            device_id=(ee, ww), device_id_type=MESH,
        ).start()

    def fold(rows):
        n = rows.shape[0]
        for j in range(TILES):
            flat[pl.ds(j, n, TILES), :] = rows[:, j * LANES : (j + 1) * LANES]
        return flat[pl.ds(0, n * TILES), :].astype(BF16).reshape(n, TILES // 2, 2, LANES)

    def unfold(rows):
        n = rows.shape[0]
        flat[pl.ds(0, n * TILES), :] = rows.astype(F32).reshape(n * TILES, LANES)
        return jnp.concatenate([flat[pl.ds(j, n, TILES), :].astype(BF16) for j in range(TILES)], axis=1)

    for copy in inputs:
        copy.wait()
    expert = iota((ALL, TOK), 0)
    match = jnp.zeros((ALL, TOK), F32)
    weight = jnp.zeros((ALL, TOK), F32)
    for k in range(ids.shape[0]):
        hit = ids[k : k + 1, :] == expert
        match = jnp.where(hit, 1.0, match)
        weight = jnp.where(hit, rw[k : k + 1, :], weight)
    earlier = jnp.where(iota((TOK, TOK), 0) < iota((TOK, TOK), 1), 1.0, 0.0).astype(BF16)
    rank = dot(match.astype(BF16), earlier)
    chosen = [jnp.where(rank == float(q), match, 0.0) for q in range(Q)]
    osend[0] = fold(dot(chosen[0].astype(BF16), tok[...]))

    pl.semaphore_wait(bar, len(near) + len(far) + len(around) + 1)

    def column_is_in():
        for dy in yorder:
            pl.semaphore_signal(column_sem, inc=1, device_id=(peer(dy, 0), w), device_id_type=MESH)

    def columns_are_in():
        pl.semaphore_wait(column_sem, len(yorder))

    def out_to(k, peers):
        q, p = k // 2, k % 2
        for dy, dz in parity(peers, p):
            remote(
                osend.at[q, peer(dy, dz)], orecv.at[k, place(e)], o_ssem, o_rsem.at[k], peer(dy, dz), w
            )

    def out_own(q):
        pltpu.make_async_copy(osend.at[q, e], orecv.at[q * 2, place(e)], o_rsem.at[q * 2]).start()

    def start_weights():
        for copy in weights:
            copy.start()
        for i, (src, dst, n) in enumerate(places):
            remote(src.at[:, 1 - core], dst.at[:, :, columns(n)], w_ssem.at[i], w_rsem.at[i], e, partner)

    def weights_here():
        for copy in weights:
            copy.wait()
        for i, (src, dst, n) in enumerate(places):
            wait_bytes(dst.at[:, :, pl.ds(0, FF)], w_rsem.at[i])

    def out_x(k):
        wait_bytes(orecv.at[k], o_rsem.at[k])
        xall[k, x] = unfold(orecv[k])
        ref = xall.at[k, x]
        for i, xx in enumerate(around):
            remote(ref, ref, x_ssem, x_rsem.at[k, i], e, xx * 2 + core)

    def project(k, xx):
        return dot(xall[k, xx], wgu[xx])

    def gathered(k):
        total = project(k, x)
        for i, xx in ((0, xl), (1, xr), (2, xo)):
            wait_bytes(xall.at[k, xx], x_rsem.at[k, i])
            total = total + project(k, xx)
        part[k] = total
        remote(part.at[k], other.at[k], p_ssem, p_rsem.at[k], e, partner)

    def back_x(k):
        wait_bytes(other.at[k], p_rsem.at[k])
        total = part[k] + other[k]
        gate, up = total[:, :CHIP], total[:, CHIP:]
        hidden = (gate / (1.0 + jnp.exp(-gate)) * up).astype(BF16)
        for i, xx in enumerate(around):
            rsend[k, i] = dot(hidden, wd[xx], ((1,), (1,))).astype(BF16)
            remote(rsend.at[k, i], rrecv.at[k, i], r_ssem, r_rsem.at[k, i], e, xx * 2 + core)
        mine[k] = dot(hidden, wd[x], ((1,), (1,)))

    def back(k):
        total = mine[k]
        for i in (0, 1, 2):
            wait_bytes(rrecv.at[k, i], r_rsem.at[k, i])
            total = total + rrecv[k, i].astype(F32)
        dsend[k] = fold(total)
        q, p = k // 2, k % 2
        for dy, dz in parity(far, p) + parity(near, p):
            to = peer(dy, dz)
            remote(dsend.at[k, place(to)], drecv.at[q, e], d_ssem, d_rsem.at[q], to, w)
        if p == 0:
            pltpu.make_async_copy(dsend.at[k, place(e)], drecv.at[q, e], d_rsem.at[q]).start()

    def combine(q):
        wait_bytes(drecv.at[q], d_rsem.at[q])
        returned = unfold(drecv[q])
        total = sum(dot(c, returned, ((0,), (0,))) for c in coeffs[q])
        if q > 0:
            total = total + mixed[...]
        if q < Q - 1:
            mixed[...] = total
        else:
            out[...] = total.astype(BF16)

    out_to(0, far + near)
    out_own(0)
    out_to(1, far + near)
    osend[1] = fold(dot(chosen[1].astype(BF16), tok[...]))
    out_to(2, far + near)
    out_own(1)
    out_to(3, far + near)
    start_weights()
    coeffs = []
    for q in range(Q):
        high = (weight * chosen[q]).astype(BF16)
        coeffs.append((high, (weight * chosen[q] - high.astype(F32)).astype(BF16)))
    for k in range(K):
        out_x(k)
    weights_here()
    gathered(0)
    for k in range(1, K):
        gathered(k)
        back_x(k - 1)
    back_x(K - 1)
    for k in range(K):
        back(k)
    for q in range(Q):
        combine(q)

    for i, (src, dst, n) in enumerate(places):
        wait_bytes(src.at[:, 1 - core], w_ssem.at[i])
    wait_bytes(osend.at[:, pl.ds(0, ALL - 1)], o_ssem)
    wait_bytes(xall.at[:, pl.ds(0, X - 1)], x_ssem)
    wait_bytes(part, p_ssem)
    wait_bytes(rsend, r_ssem)
    wait_bytes(drecv.at[:, pl.ds(0, ALL - 1)], d_ssem)


def body(tokens, expert_ids, route_weight, gate_weight, up_weight, down_weight):
    vmem = pl.BlockSpec(memory_space=pltpu.VMEM)
    hbm = pl.BlockSpec(memory_space=pl.ANY)
    dma = pltpu.SemaphoreType.DMA
    lying = (TILES // 2, 2, LANES)
    return pl.pallas_call(
        kernel,
        out_shape=jax.ShapeDtypeStruct((TOK, FEAT), BF16),
        in_specs=[hbm] * 6,
        out_specs=vmem,
        scratch_shapes=[
            pltpu.VMEM((TOK, FEAT), BF16),
            pltpu.VMEM(expert_ids.T.shape, jnp.int32),
            pltpu.VMEM(route_weight.T.shape, F32),
            pltpu.VMEM((X, FEAT, 2 * CHIP), BF16),
            pltpu.VMEM((X, FEAT, CHIP), BF16),
            pltpu.VMEM((ALL * TILES, LANES), F32),
            pltpu.VMEM((Q, ALL, *lying), BF16),
            pltpu.VMEM((K, ROWS, *lying), BF16),
            pltpu.VMEM((K, X, ROWS, FEAT), BF16),
            pltpu.VMEM((K, ROWS, 2 * CHIP), F32),
            pltpu.VMEM((K, ROWS, 2 * CHIP), F32),
            pltpu.VMEM((K, X - 1, ROWS, FEAT), BF16),
            pltpu.VMEM((K, X - 1, ROWS, FEAT), BF16),
            pltpu.VMEM((K, ROWS, FEAT), F32),
            pltpu.VMEM((K, ROWS, *lying), BF16),
            pltpu.VMEM((Q, ALL, *lying), BF16),
            pltpu.VMEM((TOK, FEAT), F32),
            dma((3,)), dma((3,)), dma((3,)), dma((3,)), pltpu.SemaphoreType.REGULAR,
            dma, dma((K,)), dma, dma((K, X - 1)), dma, dma((K,)),
            dma, dma((K, X - 1)), dma, dma((Q,)),
        ],
        compiler_params=pltpu.CompilerParams(
            collective_id=0, has_side_effects=True, vmem_limit_bytes=60 * 2**20
        ),
        cost_estimate=pl.CostEstimate(
            flops=12 * ALL * X * 2 * FEAT * FF, bytes_accessed=12 * X * FEAT * FF, transcendentals=2 * ALL * CHIP
        ),
        name="experts",
    )(
        tokens, expert_ids.T, route_weight.T,
        *(a.reshape(X, 2, FEAT, FF) for a in (gate_weight, up_weight, down_weight)),
    )


def solution(mesh):
    in_specs = (
        P("expert", "width"),
        P("expert", None),
        P("expert", None),
        P("expert", None, "width"),
        P("expert", None, "width"),
        P("expert", None, "width"),
    )
    out_specs = P("expert", "width")
    return jax.shard_map(body, mesh=mesh, in_specs=in_specs, out_specs=out_specs, check_vma=False)
```
